32 devices in a mesh: groups: 2 (over y), dp: 4 (over z), tensor: 4 (over x, core).
Axes of the slice: x: 2, y: 2, z: 4, core: 2. Of those that a mesh axis runs over, the one named last changes fastest.
Arguments:
- activations: bfloat16 [2048, 16384], P(('groups', 'dp'), 'tensor'), parts along dimension 0, may hold values from -6 to 6
- out_grads: bfloat16 [2048, 8192], P(('groups', 'dp'), 'tensor'), parts along dimension 0, may hold values from -6 to 6
- eigen_in: bfloat16 [32, 512, 512], P('tensor'), may hold values from -0.25 to 0.25
- eigen_out: bfloat16 [16, 512, 512], P('tensor'), may hold values from -0.25 to 0.25
- feature_order: int32 [4, 4096], P('tensor'), may hold values from 0 to 4095, each once within a row
- query_left: bfloat16 [32, 4, 8192], P('dp', None, 'tensor'), may hold values from -0.0625 to 0.0625
- query_right: bfloat16 [32, 4, 16384], P('dp', None, 'tensor'), may hold values from -0.046875 to 0.046875
- owner_plan: int32 [4], replicated, may hold values from 0 to 3, each once
- example_slot: int32 [2048], P(('groups', 'dp')), parts along dimension 0, may hold values from 0 to 15
Outputs:
- scores: float32 [128, 32], P(('groups', 'dp'), 'tensor'), parts along dimension 0
The draws below stay inside these ranges and needn't reach their ends.
There are 2 independent parts, one for each index of `groups`. The reference program is written for one: setup_inputs(seed, part) draws one part's arguments, and reference() takes and returns one part's arrays. A program takes and returns all parts, laid end to end along the dimension named above; an argument that names none is the same for every part. Nothing has to cross between parts.
All inputs are finite; a program needn't handle non-finite values.
Results may differ from the reference program's by a relative error of at most 0.004.
Values may be sent and summed in bfloat16 or wider, within the bound.
A program may use at most 64 MiB of HBM per device.

```python
import jax
import jax.numpy as jnp
from jax import lax

D = 8192
FF = 16384
BLK = 512
RANK = 4
QP_DEV = 8
TOK_DEV = 256
EX_DEV = 16
TOKENS = 1024
EXAMPLES = 64
QUERIES = 32
N_DP = 4
N_TENSOR = 4


def set_ends(drawn, key, low, top_value):
    shape = drawn.shape
    index_at = [jax.random.randint(jax.random.fold_in(key, axis), (), 0, shape[axis]) for axis in range(len(shape))]
    drawn = drawn.at[tuple(index_at)].set(low)
    longest = shape.index(max(shape))
    index_at[longest] = (index_at[longest] + 1) % shape[longest]
    return drawn.at[tuple(index_at)].set(top_value)


def block_levels(stream_key, shape, cuts, smallest, top_value):
    loudness, own = 1.0, jax.random.fold_in(stream_key, 6)
    for dim, shards_of in cuts:
        draws = jnp.exp(jax.random.uniform(jax.random.fold_in(own, dim), (shards_of,), jnp.float32, smallest / len(cuts), top_value / len(cuts)))
        loudness = loudness * jnp.repeat(draws, shape[dim] // shards_of).reshape([-1 if axis == dim else 1 for axis in range(len(shape))])
    return loudness


def noise(own_key, shape, width, reach, cuts=(), kind=jnp.bfloat16):
    level = block_levels(own_key, shape, cuts, -0.22, 0.18) if cuts else 1.0
    drawn = jax.random.normal(own_key, shape, jnp.float32) * width * level
    return jnp.minimum(jnp.maximum(drawn, -reach), reach).astype(kind)


def setup_inputs(seed: int = 0, part: int = 0) -> dict:
    key_list = jax.random.split(jax.random.key(seed), 10)
    part_keys = jax.random.split(jax.random.fold_in(key_list[9], part), 10)
    return {
        "activations": noise(part_keys[0], (TOKENS, FF), 1.0, 6.0, ((0, 4), (1, 4))),
        "out_grads": noise(part_keys[1], (TOKENS, D), 1.0, 6.0, ((0, 4), (1, 4))),
        "eigen_in": noise(key_list[2], (FF // BLK, BLK, BLK), BLK ** -0.5, 0.25, ((0, 4),)),
        "eigen_out": noise(key_list[3], (D // BLK, BLK, BLK), BLK ** -0.5, 0.25, ((0, 4),)),
        "feature_order": jax.vmap(lambda own: jax.random.permutation(own, FF // N_TENSOR))(jax.random.split(key_list[4], N_TENSOR)).reshape((N_TENSOR, FF // N_TENSOR)).astype(jnp.int32),
        "query_left": noise(key_list[5], (QUERIES, RANK, D), D ** -0.5, 0.0625, ((0, 4), (2, 4))),
        "query_right": noise(key_list[6], (QUERIES, RANK, FF), FF ** -0.5, 0.046875, ((0, 4), (2, 4))),
        "owner_plan": jax.random.permutation(key_list[7], N_DP).astype(jnp.int32),
        "example_slot": set_ends(jax.random.randint(part_keys[8], (TOKENS,), 0, EX_DEV), jax.random.fold_in(part_keys[8], 1), 0, EX_DEV - 1).astype(jnp.int32),
    }


def reference(activations, out_grads, eigen_in, eigen_out, feature_order, query_left, query_right, owner_plan, example_slot):
    row_count = activations.shape[0]
    shard_width = FF // N_TENSOR
    shard_base = (jnp.arange(N_TENSOR, dtype=jnp.int32) * shard_width)[:, None]
    column_index = (feature_order.astype(jnp.int32) + shard_base).reshape(FF)
    ordered_acts = jnp.take(activations, column_index, axis=1)
    rotated_acts = jnp.einsum("tbi,bij->tbj", ordered_acts.reshape(row_count, FF // BLK, BLK).astype(jnp.float32),
                              eigen_in.astype(jnp.float32), precision=lax.Precision.HIGHEST)
    rotated_acts = rotated_acts.astype(jnp.bfloat16).reshape(row_count, FF)
    rotated_grads = jnp.einsum("tbi,bij->tbj", out_grads.reshape(row_count, D // BLK, BLK).astype(jnp.float32),
                               eigen_out.astype(jnp.float32), precision=lax.Precision.HIGHEST)
    rotated_grads = rotated_grads.astype(jnp.bfloat16).reshape(row_count, D)
    left_rows = query_left.reshape(N_DP, QP_DEV, RANK, D)[owner_plan].reshape(QUERIES * RANK, D)
    right_rows = query_right.reshape(N_DP, QP_DEV, RANK, FF)[owner_plan].reshape(QUERIES * RANK, FF)
    left_proj = jnp.dot(rotated_grads, left_rows.T, preferred_element_type=jnp.float32)
    right_proj = jnp.dot(rotated_acts, right_rows.T, preferred_element_type=jnp.float32)
    token_scores = (left_proj * right_proj).reshape(row_count, QUERIES, RANK).sum(axis=2)
    slots = example_slot.reshape(N_DP, TOK_DEV)
    one_hot = (slots[:, None, :] == jnp.arange(EX_DEV, dtype=jnp.int32)[None, :, None]).astype(jnp.float32)
    scores = jnp.einsum("det,dtq->deq", one_hot, token_scores.reshape(N_DP, TOK_DEV, QUERIES),
                        precision=lax.Precision.HIGHEST)
    return scores.reshape(EXAMPLES, QUERIES)
```

```python
import functools

import jax
import jax.numpy as jnp
from jax import lax
from jax.experimental import pallas as pl
from jax.experimental.pallas import tpu as pltpu
from jax.sharding import PartitionSpec as P

EX_DEV = 16
MESH = pl.DeviceIdType.MESH
NT = (((1,), (1,)), ((), ()))


def kernel(
    dims,
    plan_ref,
    order_ref,
    slot_ref,
    acts_hbm,
    grads_hbm,
    ein_hbm,
    eout_hbm,
    query_hbm,
    out_ref,
    acts,
    grads,
    ein,
    eout,
    panels,
    rot,
    parts,
    send_buf,
    recv_buf,
    load_sem,
    zsend_sem,
    zrecv_sem,
    ysend_sem,
    yrecv_sem,
    tsend_sem,
    trecv_sem,
):
    dp, tensor, groups, chunks = dims
    y = lax.axis_index("groups")
    z = lax.axis_index("dp")
    x = lax.axis_index("tensor")
    other = groups - 1 - y
    panel_rows = panels.shape[1]
    half = panel_rows // groups
    width = panels.shape[2] // chunks
    left_width = grads.shape[1]
    right_width = acts.shape[1]
    blk = ein.shape[1]
    share = dp // tensor

    loads = [
        pltpu.make_async_copy(query_hbm, panels.at[z], load_sem.at[0]),
        pltpu.make_async_copy(grads_hbm, grads, load_sem.at[1]),
        pltpu.make_async_copy(eout_hbm, eout, load_sem.at[2]),
        pltpu.make_async_copy(acts_hbm, acts, load_sem.at[3]),
        pltpu.make_async_copy(ein_hbm, ein, load_sem.at[4]),
    ]
    for load in loads:
        load.start()

    barrier = pltpu.get_barrier_semaphore()
    has_up = z + 1 < dp
    has_down = z > 0

    @pl.when(has_up)
    def _():
        pl.semaphore_signal(barrier, inc=1, device_id={"dp": z + 1}, device_id_type=MESH)

    @pl.when(has_down)
    def _():
        pl.semaphore_signal(barrier, inc=1, device_id={"dp": z - 1}, device_id_type=MESH)

    pl.semaphore_signal(barrier, inc=1, device_id={"groups": other}, device_id_type=MESH)
    for hop in range(1, tensor):
        pl.semaphore_signal(
            barrier, inc=1, device_id={"tensor": lax.rem(x + hop, tensor)}, device_id_type=MESH
        )
    edge = jnp.where(has_up, 1, 0) + jnp.where(has_down, 1, 0)
    pl.semaphore_wait(barrier, tensor + edge)

    def piece(panel, group, chunk):
        rows = pl.ds(pl.multiple_of(group * half, half), half)
        return panels.at[panel, rows, pl.ds(chunk * width, width)]

    def z_copy(up, panel, chunk):
        ref = piece(panel, y, chunk)
        return pltpu.make_async_remote_copy(
            src_ref=ref,
            dst_ref=ref,
            send_sem=zsend_sem.at[0 if up else 1, panel, chunk],
            recv_sem=zrecv_sem.at[panel, chunk],
            device_id={"dp": z + 1 if up else z - 1},
            device_id_type=MESH,
        )

    def y_copy(panel, group, chunk):
        ref = piece(panel, group, chunk)
        return pltpu.make_async_remote_copy(
            src_ref=ref,
            dst_ref=ref,
            send_sem=ysend_sem.at[panel, chunk],
            recv_sem=yrecv_sem.at[panel, chunk],
            device_id={"groups": other},
            device_id_type=MESH,
        )

    loads[0].wait()
    for chunk in range(chunks):

        @pl.when(has_up)
        def _():
            z_copy(True, z, chunk).start()

        @pl.when(has_down)
        def _():
            z_copy(False, z, chunk).start()

    def relay(step, chunk):
        for up in (True, False):
            panel = z - step if up else z + step
            valid = panel >= 0 if up else panel < dp
            onward = has_up if up else has_down

            @pl.when(valid)
            def _():
                copy = z_copy(up, panel, chunk)
                copy.wait_recv()

                @pl.when(onward)
                def _():
                    copy.start()

                y_copy(panel, y, chunk).start()

    def rotate_left(block):
        cols = slice(block * blk, (block + 1) * blk)
        turned = jnp.dot(grads[:, cols], eout[block], preferred_element_type=jnp.float32)
        rot[:, cols] = turned.astype(jnp.bfloat16)

    def rotate_right(block):
        cols = slice(block * blk, (block + 1) * blk)
        wanted = order_ref[:, cols]
        depth = min(1024, right_width)
        total = None
        for base in range(0, right_width, depth):
            index = lax.broadcasted_iota(jnp.int32, (depth, blk), 0) + base
            picks = jnp.where(index == wanted, 1.0, 0.0).astype(jnp.bfloat16)
            term = jnp.dot(
                acts[:, base : base + depth], picks, preferred_element_type=jnp.float32
            )
            total = term if total is None else total + term
        ordered = total.astype(jnp.bfloat16)
        turned = jnp.dot(ordered, ein[block], preferred_element_type=jnp.float32)
        rot[:, left_width + block * blk : left_width + (block + 1) * blk] = turned.astype(
            jnp.bfloat16
        )

    relays = [(step, chunk) for step in range(1, dp) for chunk in range(chunks)]
    work = [(rotate_left, block) for block in range(eout.shape[0])]
    work += [(rotate_right, block) for block in range(ein.shape[0])]
    done = 0
    for index, (job, block) in enumerate(work):
        if index == 0:
            loads[1].wait()
            loads[2].wait()
        if index == eout.shape[0]:
            loads[3].wait()
            loads[4].wait()
        job(block)
        until = (index + 1) * len(relays) // len(work)
        for step, chunk in relays[done:until]:
            relay(step, chunk)
        done = until

    def each_foreign(body):
        for step in range(1, dp):
            for up in (True, False):
                panel = z - step if up else z + step
                valid = panel >= 0 if up else panel < dp

                @pl.when(valid)
                def _():
                    for chunk in range(chunks):
                        body(up, panel, chunk)

    each_foreign(lambda up, panel, chunk: y_copy(panel, other, chunk).wait_recv())

    for panel in range(dp):
        parts[0, panel] = lax.dot_general(
            panels[panel, :, :left_width], rot[:, :left_width], NT, preferred_element_type=jnp.float32
        )
        parts[1, panel] = lax.dot_general(
            panels[panel, :, left_width:], rot[:, left_width:], NT, preferred_element_type=jnp.float32
        )

    def gather_share(hop):
        target = lax.rem(x + hop, tensor)
        for place in range(share):
            owner = plan_ref[target * share + place]
            for side in range(2):
                total = jnp.zeros_like(parts[side, 0])
                for panel in range(dp):
                    total = jnp.where(owner == panel, parts[side, panel], total)
                send_buf[hop, side, place * panel_rows : (place + 1) * panel_rows] = total

    def t_copy(hop):
        return pltpu.make_async_remote_copy(
            src_ref=send_buf.at[hop],
            dst_ref=recv_buf.at[hop],
            send_sem=tsend_sem.at[hop],
            recv_sem=trecv_sem.at[hop],
            device_id={"tensor": lax.rem(x + hop, tensor)},
            device_id_type=MESH,
        )

    for hop in range(1, tensor):
        gather_share(hop)
        t_copy(hop).start()
    gather_share(0)
    left = send_buf[0, 0]
    right = send_buf[0, 1]

    @pl.when(has_up)
    def _():
        for chunk in range(chunks):
            z_copy(True, z, chunk).wait_send()

    @pl.when(has_down)
    def _():
        for chunk in range(chunks):
            z_copy(False, z, chunk).wait_send()

    def drain(up, panel, chunk):
        y_copy(panel, y, chunk).wait_send()

        @pl.when(has_up if up else has_down)
        def _():
            z_copy(up, panel, chunk).wait_send()

    each_foreign(drain)

    for hop in range(1, tensor):
        t_copy(hop).wait()
        left += recv_buf[hop, 0]
        right += recv_buf[hop, 1]
    product = left * right
    examples = lax.broadcasted_iota(jnp.int32, (EX_DEV, slot_ref.shape[1]), 0)
    one_hot = jnp.where(examples == slot_ref[...], 1.0, 0.0).astype(jnp.float32)
    sums = lax.dot_general(
        one_hot, product, NT, precision=lax.Precision.HIGHEST, preferred_element_type=jnp.float32
    )
    queries = out_ref.shape[1]
    rank = sums.shape[1] // queries
    row = lax.broadcasted_iota(jnp.int32, (sums.shape[1], queries), 0)
    col = lax.broadcasted_iota(jnp.int32, (sums.shape[1], queries), 1)
    fold = jnp.where((row >= col * rank) & (row < (col + 1) * rank), 1.0, 0.0).astype(jnp.float32)
    out_ref[...] = jnp.dot(
        sums, fold, precision=lax.Precision.HIGHEST, preferred_element_type=jnp.float32
    )


def local(
    activations,
    out_grads,
    eigen_in,
    eigen_out,
    feature_order,
    query_left,
    query_right,
    owner_plan,
    example_slot,
):
    dp = lax.axis_size("dp")
    tensor = lax.axis_size("tensor")
    groups = lax.axis_size("groups")
    tokens, right_width = activations.shape
    left_width = out_grads.shape[1]
    panel_rows = query_left.shape[0] * query_left.shape[1]
    width = left_width + right_width
    query = jnp.concatenate([query_left, query_right], axis=2).reshape(panel_rows, width)
    chunks = 3
    share = dp // tensor
    bf16, f32 = jnp.bfloat16, jnp.float32
    vmem = pl.BlockSpec(memory_space=pltpu.VMEM)
    anywhere = pl.BlockSpec(memory_space=pl.ANY)
    dma = pltpu.SemaphoreType.DMA
    return pl.pallas_call(
        functools.partial(kernel, (dp, tensor, groups, chunks)),
        out_shape=jax.ShapeDtypeStruct((EX_DEV, share * query_left.shape[0]), f32),
        in_specs=[pl.BlockSpec(memory_space=pltpu.SMEM), vmem, vmem] + [anywhere] * 5,
        out_specs=vmem,
        scratch_shapes=[
            pltpu.VMEM(activations.shape, bf16),
            pltpu.VMEM(out_grads.shape, bf16),
            pltpu.VMEM(eigen_in.shape, bf16),
            pltpu.VMEM(eigen_out.shape, bf16),
            pltpu.VMEM((dp, panel_rows, width), bf16),
            pltpu.VMEM((tokens, width), bf16),
            pltpu.VMEM((2, dp, panel_rows, tokens), f32),
            pltpu.VMEM((tensor, 2, share * panel_rows, tokens), f32),
            pltpu.VMEM((tensor, 2, share * panel_rows, tokens), f32),
            dma((5,)),
            dma((2, dp, chunks)),
            dma((dp, chunks)),
            dma((dp, chunks)),
            dma((dp, chunks)),
            dma((tensor,)),
            dma((tensor,)),
        ],
        compiler_params=pltpu.CompilerParams(
            collective_id=0, has_side_effects=True, vmem_limit_bytes=56 * 1024 * 1024
        ),
    )(
        owner_plan,
        feature_order,
        example_slot[None, :],
        activations,
        out_grads,
        eigen_in,
        eigen_out,
        query,
    )


def solution(mesh):
    placed = (
        P(("groups", "dp"), "tensor"),
        P(("groups", "dp"), "tensor"),
        P("tensor", None, None),
        P("tensor", None, None),
        P("tensor", None),
        P("dp", None, "tensor"),
        P("dp", None, "tensor"),
        P(),
        P(("groups", "dp")),
    )
    return jax.shard_map(
        local, mesh=mesh, in_specs=placed, out_specs=P(("groups", "dp"), "tensor"), check_vma=False
    )
```

```python
import functools

import jax
import jax.numpy as jnp
from jax import lax
from jax.experimental import pallas as pl
from jax.experimental.pallas import tpu as pltpu
from jax.sharding import PartitionSpec as P

EX_DEV = 16
MESH = pl.DeviceIdType.MESH
NT = (((1,), (1,)), ((), ()))


def kernel(
    dims,
    plan_ref,
    order_ref,
    slot_ref,
    acts_hbm,
    grads_hbm,
    ein_hbm,
    eout_hbm,
    ql_hbm,
    qr_hbm,
    out_ref,
    acts,
    grads,
    ein,
    eout,
    ql_stage,
    qr_stage,
    wide,
    ordered,
    panels,
    rot,
    parts,
    send_buf,
    recv_buf,
    load_sem,
    zsend_sem,
    zrecv_sem,
    ysend_sem,
    yrecv_sem,
    tsend_sem,
    trecv_sem,
):
    dp, tensor, groups, chunks = dims
    y = lax.axis_index("groups")
    z = lax.axis_index("dp")
    x = lax.axis_index("tensor")
    other = groups - 1 - y
    panel_rows = panels.shape[1]
    half = panel_rows // groups
    width = panels.shape[2] // chunks
    left_width = grads.shape[1]
    right_width = acts.shape[1]
    blk = ein.shape[1]
    share = dp // tensor

    loads = [
        pltpu.make_async_copy(ql_hbm, ql_stage, load_sem.at[0]),
        pltpu.make_async_copy(qr_hbm, qr_stage, load_sem.at[1]),
        pltpu.make_async_copy(grads_hbm, grads, load_sem.at[2]),
        pltpu.make_async_copy(eout_hbm, eout, load_sem.at[3]),
        pltpu.make_async_copy(acts_hbm, acts, load_sem.at[4]),
        pltpu.make_async_copy(ein_hbm, ein, load_sem.at[5]),
    ]
    for load in loads:
        load.start()

    barrier = pltpu.get_barrier_semaphore()
    has_up = z + 1 < dp
    has_down = z > 0

    @pl.when(has_up)
    def _():
        pl.semaphore_signal(barrier, inc=1, device_id={"dp": z + 1}, device_id_type=MESH)

    @pl.when(has_down)
    def _():
        pl.semaphore_signal(barrier, inc=1, device_id={"dp": z - 1}, device_id_type=MESH)

    pl.semaphore_signal(barrier, inc=1, device_id={"groups": other}, device_id_type=MESH)
    for hop in range(1, tensor):
        pl.semaphore_signal(
            barrier, inc=1, device_id={"tensor": lax.rem(x + hop, tensor)}, device_id_type=MESH
        )
    def piece(panel, group, chunk):
        rows = pl.ds(pl.multiple_of(group * half, half), half)
        return panels.at[panel, rows, pl.ds(chunk * width, width)]

    def z_copy(up, panel, chunk):
        ref = piece(panel, y, chunk)
        return pltpu.make_async_remote_copy(
            src_ref=ref,
            dst_ref=ref,
            send_sem=zsend_sem.at[0 if up else 1, panel, chunk],
            recv_sem=zrecv_sem.at[panel, chunk],
            device_id={"dp": z + 1 if up else z - 1},
            device_id_type=MESH,
        )

    def y_copy(panel, group, chunk):
        ref = piece(panel, group, chunk)
        return pltpu.make_async_remote_copy(
            src_ref=ref,
            dst_ref=ref,
            send_sem=ysend_sem.at[panel, chunk],
            recv_sem=yrecv_sem.at[panel, chunk],
            device_id={"groups": other},
            device_id_type=MESH,
        )

    rank = ql_stage.shape[1]

    def stage(source, base):
        for query in range(source.shape[0]):
            wide[query * rank : (query + 1) * rank, base : base + source.shape[2]] = source[
                query
            ].astype(jnp.float32)
        span = slice(base, base + source.shape[2])
        panels[z, :, span] = wide[:, span].astype(jnp.bfloat16)

    def launch(chunk):
        @pl.when(has_up)
        def _():
            z_copy(True, z, chunk).start()

        @pl.when(has_down)
        def _():
            z_copy(False, z, chunk).start()

    loads[0].wait()
    stage(ql_stage, 0)
    edge = jnp.where(has_up, 1, 0) + jnp.where(has_down, 1, 0)
    pl.semaphore_wait(barrier, tensor + edge)
    ahead = 2
    left_chunks = left_width // width
    for chunk in range(min(ahead, left_chunks)):
        launch(chunk)
    loads[1].wait()
    stage(qr_stage, left_width)
    for chunk in range(left_chunks, ahead):
        launch(chunk)

    def relay(step, chunk):
        for up in (True, False):
            panel = z - step if up else z + step
            valid = panel >= 0 if up else panel < dp
            onward = has_up if up else has_down

            @pl.when(valid)
            def _():
                copy = z_copy(up, panel, chunk)
                copy.wait_recv()

                @pl.when(onward)
                def _():
                    copy.start()

                y_copy(panel, y, chunk).start()

    def rotate_left(block):
        cols = slice(block * blk, (block + 1) * blk)
        turned = jnp.dot(grads[:, cols], eout[block], preferred_element_type=jnp.float32)
        rot[:, cols] = turned.astype(jnp.bfloat16)

    parts_per_block = 2

    def order_columns(block, part):
        span = blk // parts_per_block
        cols = slice(block * blk + part * span, block * blk + (part + 1) * span)
        wanted = order_ref[:, cols]
        depth = min(1024, right_width)
        total = None
        for base in range(0, right_width, depth):
            index = lax.broadcasted_iota(jnp.int32, (depth, span), 0) + base
            picks = jnp.where(index == wanted, 1.0, 0.0).astype(jnp.bfloat16)
            term = jnp.dot(
                acts[:, base : base + depth], picks, preferred_element_type=jnp.float32
            )
            total = term if total is None else total + term
        ordered[:, part * span : (part + 1) * span] = total.astype(jnp.bfloat16)
        if part == parts_per_block - 1:
            turned = jnp.dot(ordered[...], ein[block], preferred_element_type=jnp.float32)
            start = left_width + block * blk
            rot[:, start : start + blk] = turned.astype(jnp.bfloat16)

    def arrive(step, chunk):
        for up in (True, False):
            panel = z - step if up else z + step

            @pl.when(panel >= 0 if up else panel < dp)
            def _():
                y_copy(panel, other, chunk).wait_recv()

    def project(chunk):
        side = 0 if chunk < left_chunks else 1
        cols = slice(chunk * width, (chunk + 1) * width)
        term = lax.dot_general(
            panels[:, :, cols].reshape(dp * panel_rows, width),
            rot[:, cols],
            NT,
            preferred_element_type=jnp.float32,
        ).reshape(parts.shape[1:])
        if chunk in (0, left_chunks):
            parts[side] = term
        else:
            parts[side] += term

    def gather_share(hop, side):
        target = lax.rem(x + hop, tensor)
        for place in range(share):
            owner = plan_ref[target * share + place]
            total = jnp.zeros_like(parts[side, 0])
            for panel in range(dp):
                total = jnp.where(owner == panel, parts[side, panel], total)
            send_buf[hop, side, place * panel_rows : (place + 1) * panel_rows] = total

    def t_copy(hop, side):
        return pltpu.make_async_remote_copy(
            src_ref=send_buf.at[hop, side],
            dst_ref=recv_buf.at[hop, side],
            send_sem=tsend_sem.at[hop, side],
            recv_sem=trecv_sem.at[hop, side],
            device_id={"tensor": lax.rem(x + hop, tensor)},
            device_id_type=MESH,
        )

    def reduce_side(side):
        for hop in [*range(1, tensor), 0]:
            gather_share(hop, side)
            if hop:
                t_copy(hop, side).start()

    work = [(rotate_left, (block,)) for block in range(eout.shape[0])]
    work += [
        (order_columns, (block, part))
        for block in range(ein.shape[0])
        for part in range(parts_per_block)
    ]
    events = [(chunk, 0, chunk) for chunk in range(ahead, chunks)]
    events += [
        (chunk + step * ahead, step, chunk) for step in range(1, dp) for chunk in range(chunks)
    ]
    events.sort()
    done = 0

    def advance(until):
        nonlocal done
        for index, (job, where) in enumerate(work[done:until], done):
            if index == 0:
                loads[2].wait()
                loads[3].wait()
            if index == eout.shape[0]:
                loads[4].wait()
                loads[5].wait()
            job(*where)
        done = max(done, until)

    def finish(chunk):
        if chunk >= left_chunks:
            last_block = (chunk + 1) * width - left_width
            advance(eout.shape[0] + parts_per_block * (-(-last_block // blk)))
        else:
            advance(eout.shape[0])
        for step in range(1, dp):
            arrive(step, chunk)
        project(chunk)
        if chunk == left_chunks - 1:
            reduce_side(0)

    lag = 2
    ready = []
    for index, (_, step, chunk) in enumerate(events):
        if step:
            advance((index + 1) * len(work) // len(events))
            relay(step, chunk)
        else:
            launch(chunk)
        if step == dp - 1 and chunk < chunks - 1:
            ready.append((index + lag, chunk))
        while ready and ready[0][0] <= index:
            finish(ready.pop(0)[1])
    for _, chunk in ready:
        finish(chunk)
    advance(len(work))
    finish(chunks - 1)
    reduce_side(1)

    def each_foreign(body):
        for step in range(1, dp):
            for up in (True, False):
                panel = z - step if up else z + step
                valid = panel >= 0 if up else panel < dp

                @pl.when(valid)
                def _():
                    for chunk in range(chunks):
                        body(up, panel, chunk)

    left = send_buf[0, 0]
    right = send_buf[0, 1]

    @pl.when(has_up)
    def _():
        for chunk in range(chunks):
            z_copy(True, z, chunk).wait_send()

    @pl.when(has_down)
    def _():
        for chunk in range(chunks):
            z_copy(False, z, chunk).wait_send()

    def drain(up, panel, chunk):
        y_copy(panel, y, chunk).wait_send()

        @pl.when(has_up if up else has_down)
        def _():
            z_copy(up, panel, chunk).wait_send()

    each_foreign(drain)

    for hop in range(1, tensor):
        for side in range(2):
            t_copy(hop, side).wait()
        left += recv_buf[hop, 0]
        right += recv_buf[hop, 1]
    product = left * right
    examples = lax.broadcasted_iota(jnp.int32, (EX_DEV, slot_ref.shape[1]), 0)
    one_hot = jnp.where(examples == slot_ref[...], 1.0, 0.0).astype(jnp.float32)
    sums = lax.dot_general(
        one_hot, product, NT, precision=lax.Precision.HIGHEST, preferred_element_type=jnp.float32
    )
    queries = out_ref.shape[1]
    row = lax.broadcasted_iota(jnp.int32, (sums.shape[1], queries), 0)
    col = lax.broadcasted_iota(jnp.int32, (sums.shape[1], queries), 1)
    fold = jnp.where((row >= col * rank) & (row < (col + 1) * rank), 1.0, 0.0).astype(jnp.float32)
    out_ref[...] = jnp.dot(
        sums, fold, precision=lax.Precision.HIGHEST, preferred_element_type=jnp.float32
    )


def local(
    activations,
    out_grads,
    eigen_in,
    eigen_out,
    feature_order,
    query_left,
    query_right,
    owner_plan,
    example_slot,
):
    dp = lax.axis_size("dp")
    tensor = lax.axis_size("tensor")
    groups = lax.axis_size("groups")
    tokens, right_width = activations.shape
    left_width = out_grads.shape[1]
    panel_rows = query_left.shape[0] * query_left.shape[1]
    width = left_width + right_width
    chunks = 3
    share = dp // tensor
    bf16, f32 = jnp.bfloat16, jnp.float32
    vmem = pl.BlockSpec(memory_space=pltpu.VMEM)
    anywhere = pl.BlockSpec(memory_space=pl.ANY)
    dma = pltpu.SemaphoreType.DMA
    return pl.pallas_call(
        functools.partial(kernel, (dp, tensor, groups, chunks)),
        out_shape=jax.ShapeDtypeStruct((EX_DEV, share * query_left.shape[0]), f32),
        in_specs=[pl.BlockSpec(memory_space=pltpu.SMEM), vmem, vmem] + [anywhere] * 6,
        out_specs=vmem,
        scratch_shapes=[
            pltpu.VMEM(activations.shape, bf16),
            pltpu.VMEM(out_grads.shape, bf16),
            pltpu.VMEM(eigen_in.shape, bf16),
            pltpu.VMEM(eigen_out.shape, bf16),
            pltpu.VMEM(query_left.shape, bf16),
            pltpu.VMEM(query_right.shape, bf16),
            pltpu.VMEM((panel_rows, width), f32),
            pltpu.VMEM((tokens, eigen_in.shape[1]), bf16),
            pltpu.VMEM((dp, panel_rows, width), bf16),
            pltpu.VMEM((tokens, width), bf16),
            pltpu.VMEM((2, dp, panel_rows, tokens), f32),
            pltpu.VMEM((tensor, 2, share * panel_rows, tokens), f32),
            pltpu.VMEM((tensor, 2, share * panel_rows, tokens), f32),
            dma((6,)),
            dma((2, dp, chunks)),
            dma((dp, chunks)),
            dma((dp, chunks)),
            dma((dp, chunks)),
            dma((tensor, 2)),
            dma((tensor, 2)),
        ],
        compiler_params=pltpu.CompilerParams(
            collective_id=0, has_side_effects=True, vmem_limit_bytes=56 * 1024 * 1024
        ),
    )(
        owner_plan,
        feature_order,
        example_slot[None, :],
        activations,
        out_grads,
        eigen_in,
        eigen_out,
        query_left,
        query_right,
    )


def solution(mesh):
    placed = (
        P(("groups", "dp"), "tensor"),
        P(("groups", "dp"), "tensor"),
        P("tensor", None, None),
        P("tensor", None, None),
        P("tensor", None),
        P("dp", None, "tensor"),
        P("dp", None, "tensor"),
        P(),
        P(("groups", "dp")),
    )
    return jax.shard_map(
        local, mesh=mesh, in_specs=placed, out_specs=P(("groups", "dp"), "tensor"), check_vma=False
    )
```

```python
import functools

import jax
import jax.numpy as jnp
from jax import lax
from jax.experimental import pallas as pl
from jax.experimental.pallas import tpu as pltpu
from jax.sharding import PartitionSpec as P

EX_DEV = 16
MESH = pl.DeviceIdType.MESH
NT = (((1,), (1,)), ((), ()))


def kernel(
    dims,
    plan_ref,
    order_ref,
    slot_ref,
    acts_hbm,
    grads_hbm,
    ein_hbm,
    eout_hbm,
    ql_hbm,
    qr_hbm,
    out_ref,
    acts,
    grads,
    ein,
    eout,
    ql_stage,
    qr_stage,
    wide,
    ordered,
    panels,
    rot,
    parts,
    send_buf,
    recv_buf,
    load_sem,
    zsend_sem,
    zrecv_sem,
    ysend_sem,
    yrecv_sem,
    tsend_sem,
    trecv_sem,
):
    dp, tensor, groups, chunks = dims
    y = lax.axis_index("groups")
    z = lax.axis_index("dp")
    x = lax.axis_index("tensor")
    other = groups - 1 - y
    panel_rows = panels.shape[1]
    half = panel_rows // groups
    width = panels.shape[2] // chunks
    left_width = grads.shape[1]
    right_width = acts.shape[1]
    blk = ein.shape[1]
    share = dp // tensor

    loads = [
        pltpu.make_async_copy(ql_hbm, ql_stage, load_sem.at[0]),
        pltpu.make_async_copy(qr_hbm, qr_stage, load_sem.at[1]),
        pltpu.make_async_copy(grads_hbm, grads, load_sem.at[2]),
        pltpu.make_async_copy(eout_hbm, eout, load_sem.at[3]),
        pltpu.make_async_copy(acts_hbm, acts, load_sem.at[4]),
        pltpu.make_async_copy(ein_hbm, ein, load_sem.at[5]),
    ]
    for load in loads:
        load.start()

    barrier = pltpu.get_barrier_semaphore()
    has_up = z + 1 < dp
    has_down = z > 0

    @pl.when(has_up)
    def _():
        pl.semaphore_signal(barrier, inc=1, device_id={"dp": z + 1}, device_id_type=MESH)

    @pl.when(has_down)
    def _():
        pl.semaphore_signal(barrier, inc=1, device_id={"dp": z - 1}, device_id_type=MESH)

    pl.semaphore_signal(barrier, inc=1, device_id={"groups": other}, device_id_type=MESH)
    for hop in range(1, tensor):
        pl.semaphore_signal(
            barrier, inc=1, device_id={"tensor": lax.rem(x + hop, tensor)}, device_id_type=MESH
        )
    def piece(panel, group, chunk):
        rows = pl.ds(pl.multiple_of(group * half, half), half)
        return panels.at[panel, rows, pl.ds(chunk * width, width)]

    def z_copy(up, panel, chunk):
        ref = piece(panel, y, chunk)
        return pltpu.make_async_remote_copy(
            src_ref=ref,
            dst_ref=ref,
            send_sem=zsend_sem.at[0 if up else 1, panel, chunk],
            recv_sem=zrecv_sem.at[panel, chunk],
            device_id={"dp": z + 1 if up else z - 1},
            device_id_type=MESH,
        )

    def y_copy(panel, group, chunk):
        ref = piece(panel, group, chunk)
        return pltpu.make_async_remote_copy(
            src_ref=ref,
            dst_ref=ref,
            send_sem=ysend_sem.at[panel, chunk],
            recv_sem=yrecv_sem.at[panel, chunk],
            device_id={"groups": other},
            device_id_type=MESH,
        )

    rank = ql_stage.shape[1]

    def stage(source, base):
        for query in range(source.shape[0]):
            wide[query * rank : (query + 1) * rank, base : base + source.shape[2]] = source[
                query
            ].astype(jnp.float32)
        span = slice(base, base + source.shape[2])
        panels[z, :, span] = wide[:, span].astype(jnp.bfloat16)

    def launch(chunk):
        @pl.when(has_up)
        def _():
            z_copy(True, z, chunk).start()

        @pl.when(has_down)
        def _():
            z_copy(False, z, chunk).start()

    loads[0].wait()
    stage(ql_stage, 0)
    edge = jnp.where(has_up, 1, 0) + jnp.where(has_down, 1, 0)
    pl.semaphore_wait(barrier, tensor + edge)
    ahead = 2
    left_chunks = left_width // width
    for chunk in range(min(ahead, left_chunks)):
        launch(chunk)
    loads[1].wait()
    stage(qr_stage, left_width)
    for chunk in range(left_chunks, ahead):
        launch(chunk)

    def relay(step, chunk):
        for up in (True, False):
            panel = z - step if up else z + step
            valid = panel >= 0 if up else panel < dp
            onward = has_up if up else has_down

            @pl.when(valid)
            def _():
                copy = z_copy(up, panel, chunk)
                copy.wait_recv()

                @pl.when(onward)
                def _():
                    copy.start()

                y_copy(panel, y, chunk).start()

    def rotate_left(block):
        cols = slice(block * blk, (block + 1) * blk)
        turned = jnp.dot(grads[:, cols], eout[block], preferred_element_type=jnp.float32)
        rot[:, cols] = turned.astype(jnp.bfloat16)

    parts_per_block = 2

    def order_columns(block, part):
        span = blk // parts_per_block
        cols = slice(block * blk + part * span, block * blk + (part + 1) * span)
        wanted = order_ref[:, cols]
        depth = min(1024, right_width)
        total = None
        for base in range(0, right_width, depth):
            index = lax.broadcasted_iota(jnp.int32, (depth, span), 0) + base
            picks = jnp.where(index == wanted, 1.0, 0.0).astype(jnp.bfloat16)
            term = jnp.dot(
                acts[:, base : base + depth], picks, preferred_element_type=jnp.float32
            )
            total = term if total is None else total + term
        ordered[:, part * span : (part + 1) * span] = total.astype(jnp.bfloat16)
        if part == parts_per_block - 1:
            turned = jnp.dot(ordered[...], ein[block], preferred_element_type=jnp.float32)
            start = left_width + block * blk
            rot[:, start : start + blk] = turned.astype(jnp.bfloat16)

    def arrive(step, chunk):
        for up in (True, False):
            panel = z - step if up else z + step

            @pl.when(panel >= 0 if up else panel < dp)
            def _():
                y_copy(panel, other, chunk).wait_recv()

    def project(chunk):
        side = 0 if chunk < left_chunks else 1
        cols = slice(chunk * width, (chunk + 1) * width)
        term = lax.dot_general(
            panels[:, :, cols].reshape(dp * panel_rows, width),
            rot[:, cols],
            NT,
            preferred_element_type=jnp.float32,
        ).reshape(parts.shape[1:])
        if chunk in (0, left_chunks):
            parts[side] = term
        else:
            parts[side] += term

    def gather_share(hop, side):
        target = lax.rem(x + hop, tensor)
        for place in range(share):
            owner = plan_ref[target * share + place]
            total = jnp.zeros_like(parts[side, 0])
            for panel in range(dp):
                total = jnp.where(owner == panel, parts[side, panel], total)
            send_buf[hop, side, place * panel_rows : (place + 1) * panel_rows] = total

    def t_copy(hop, side):
        return pltpu.make_async_remote_copy(
            src_ref=send_buf.at[hop, side],
            dst_ref=recv_buf.at[hop, side],
            send_sem=tsend_sem.at[hop, side],
            recv_sem=trecv_sem.at[hop, side],
            device_id={"tensor": lax.rem(x + hop, tensor)},
            device_id_type=MESH,
        )

    def reduce_side(side):
        for hop in [*sorted(range(1, tensor), key=lambda hop: abs(2 * hop - tensor)), 0]:
            gather_share(hop, side)
            if hop:
                t_copy(hop, side).start()

    work = [(rotate_left, (block,)) for block in range(eout.shape[0])]
    work += [
        (order_columns, (block, part))
        for block in range(ein.shape[0])
        for part in range(parts_per_block)
    ]
    events = [(chunk, 0, chunk) for chunk in range(ahead, chunks)]
    events += [
        (chunk + step * ahead, step, chunk) for step in range(1, dp) for chunk in range(chunks)
    ]
    events.sort()
    done = 0

    def advance(until):
        nonlocal done
        for index, (job, where) in enumerate(work[done:until], done):
            if index == 0:
                loads[2].wait()
                loads[3].wait()
            if index == eout.shape[0]:
                loads[4].wait()
                loads[5].wait()
            job(*where)
        done = max(done, until)

    def finish(chunk):
        if chunk >= left_chunks:
            last_block = (chunk + 1) * width - left_width
            advance(eout.shape[0] + parts_per_block * (-(-last_block // blk)))
        else:
            advance(eout.shape[0])
        for step in range(1, dp):
            arrive(step, chunk)
        project(chunk)
        if chunk == left_chunks - 1:
            reduce_side(0)

    lag = 3
    ready = []
    for index, (_, step, chunk) in enumerate(events):
        if step:
            relay(step, chunk)
            advance((index + 1) * len(work) // len(events))
        else:
            launch(chunk)
        if step == dp - 1 and chunk < chunks - 1:
            ready.append((index + lag, chunk))
        while ready and ready[0][0] <= index:
            finish(ready.pop(0)[1])
    for _, chunk in ready:
        finish(chunk)
    advance(len(work))
    finish(chunks - 1)
    reduce_side(1)

    def each_foreign(body):
        for step in range(1, dp):
            for up in (True, False):
                panel = z - step if up else z + step
                valid = panel >= 0 if up else panel < dp

                @pl.when(valid)
                def _():
                    for chunk in range(chunks):
                        body(up, panel, chunk)

    left = send_buf[0, 0]
    right = send_buf[0, 1]

    @pl.when(has_up)
    def _():
        for chunk in range(chunks):
            z_copy(True, z, chunk).wait_send()

    @pl.when(has_down)
    def _():
        for chunk in range(chunks):
            z_copy(False, z, chunk).wait_send()

    def drain(up, panel, chunk):
        y_copy(panel, y, chunk).wait_send()

        @pl.when(has_up if up else has_down)
        def _():
            z_copy(up, panel, chunk).wait_send()

    each_foreign(drain)

    for hop in range(1, tensor):
        for side in range(2):
            t_copy(hop, side).wait()
        left += recv_buf[hop, 0]
        right += recv_buf[hop, 1]
    product = left * right
    examples = lax.broadcasted_iota(jnp.int32, (EX_DEV, slot_ref.shape[1]), 0)
    one_hot = jnp.where(examples == slot_ref[...], 1.0, 0.0).astype(jnp.float32)
    sums = lax.dot_general(
        one_hot, product, NT, precision=lax.Precision.HIGHEST, preferred_element_type=jnp.float32
    )
    queries = out_ref.shape[1]
    row = lax.broadcasted_iota(jnp.int32, (sums.shape[1], queries), 0)
    col = lax.broadcasted_iota(jnp.int32, (sums.shape[1], queries), 1)
    fold = jnp.where((row >= col * rank) & (row < (col + 1) * rank), 1.0, 0.0).astype(jnp.float32)
    out_ref[...] = jnp.dot(
        sums, fold, precision=lax.Precision.HIGHEST, preferred_element_type=jnp.float32
    )


def local(
    activations,
    out_grads,
    eigen_in,
    eigen_out,
    feature_order,
    query_left,
    query_right,
    owner_plan,
    example_slot,
):
    dp = lax.axis_size("dp")
    tensor = lax.axis_size("tensor")
    groups = lax.axis_size("groups")
    tokens, right_width = activations.shape
    left_width = out_grads.shape[1]
    panel_rows = query_left.shape[0] * query_left.shape[1]
    width = left_width + right_width
    chunks = 3
    share = dp // tensor
    bf16, f32 = jnp.bfloat16, jnp.float32
    vmem = pl.BlockSpec(memory_space=pltpu.VMEM)
    anywhere = pl.BlockSpec(memory_space=pl.ANY)
    dma = pltpu.SemaphoreType.DMA
    return pl.pallas_call(
        functools.partial(kernel, (dp, tensor, groups, chunks)),
        out_shape=jax.ShapeDtypeStruct((EX_DEV, share * query_left.shape[0]), f32),
        in_specs=[pl.BlockSpec(memory_space=pltpu.SMEM), vmem, vmem] + [anywhere] * 6,
        out_specs=vmem,
        scratch_shapes=[
            pltpu.VMEM(activations.shape, bf16),
            pltpu.VMEM(out_grads.shape, bf16),
            pltpu.VMEM(eigen_in.shape, bf16),
            pltpu.VMEM(eigen_out.shape, bf16),
            pltpu.VMEM(query_left.shape, bf16),
            pltpu.VMEM(query_right.shape, bf16),
            pltpu.VMEM((panel_rows, width), f32),
            pltpu.VMEM((tokens, eigen_in.shape[1]), bf16),
            pltpu.VMEM((dp, panel_rows, width), bf16),
            pltpu.VMEM((tokens, width), bf16),
            pltpu.VMEM((2, dp, panel_rows, tokens), f32),
            pltpu.VMEM((tensor, 2, share * panel_rows, tokens), f32),
            pltpu.VMEM((tensor, 2, share * panel_rows, tokens), f32),
            dma((6,)),
            dma((2, dp, chunks)),
            dma((dp, chunks)),
            dma((dp, chunks)),
            dma((dp, chunks)),
            dma((tensor, 2)),
            dma((tensor, 2)),
        ],
        compiler_params=pltpu.CompilerParams(
            collective_id=0, has_side_effects=True, vmem_limit_bytes=56 * 1024 * 1024
        ),
    )(
        owner_plan,
        feature_order,
        example_slot[None, :],
        activations,
        out_grads,
        eigen_in,
        eigen_out,
        query_left,
        query_right,
    )


def solution(mesh):
    placed = (
        P(("groups", "dp"), "tensor"),
        P(("groups", "dp"), "tensor"),
        P("tensor", None, None),
        P("tensor", None, None),
        P("tensor", None),
        P("dp", None, "tensor"),
        P("dp", None, "tensor"),
        P(),
        P(("groups", "dp")),
    )
    return jax.shard_map(
        local, mesh=mesh, in_specs=placed, out_specs=P(("groups", "dp"), "tensor"), check_vma=False
    )
```
